32 devices in a mesh: groups: 2 (over y), seq: 4 (over z), heads: 2 (over x), section: 2 (over core).
Axes of the slice: x: 2, y: 2, z: 4, core: 2. Of those that a mesh axis runs over, the one named last changes fastest.
Arguments:
- prefill_q: bfloat16 [16384, 8192], P(('groups', 'seq', 'section'), 'heads'), parts along dimension 0, may hold values from -16 to 16
- prefill_kv: bfloat16 [16384, 2, 1024], P(('groups', 'seq', 'section'), None, 'heads'), parts along dimension 0, may hold values from -16 to 16
- lengths: int32 [4], P('groups'), parts along dimension 0, may hold values from 1024 to 4096, as said below
- decode_q: bfloat16 [128, 4, 8192], P(('groups', 'seq'), None, 'heads'), parts along dimension 0, may hold values from -16 to 16
- decode_kv: bfloat16 [128, 4, 2, 1024], P(('groups', 'seq'), None, None, 'heads'), parts along dimension 0, may hold values from -16 to 16
- row_cand: int32 [128], P(('groups', 'seq')), parts along dimension 0, may hold values from 0 to 1, as said below
- positions: int32 [128], P(('groups', 'seq')), parts along dimension 0, may hold values from 1 to 4096, as said below
- out_weight: bfloat16 [8192, 8192], P('heads', ('seq', 'section')), may hold values from -0.0625 to 0.0625
Outputs:
- prefill_out: bfloat16 [16384, 8192], P(('groups', 'seq', 'section'), 'heads'), parts along dimension 0
- decoded: bfloat16 [128, 4, 8192], P(('groups', 'heads'), None, ('seq', 'section')), parts along dimension 0
The draws below stay inside these ranges and needn't reach their ends.
There are 2 independent parts, one for each index of `groups`. The reference program is written for one: setup_inputs(seed, part) draws one part's arguments, and reference() takes and returns one part's arrays. A program takes and returns all parts, laid end to end along the dimension named above; an argument that names none is the same for every part. Nothing has to cross between parts.
Inputs may be any that keep to these rules, and one draw needn't show every extreme that they name: `lengths`: each candidate's tokens sit at positions below its length; one candidate is full. `row_cand`: every candidate is continued by some row. `positions`: A row's count is at most the length of its candidate.
All inputs are finite; a program needn't handle non-finite values.
Results may differ from the reference program's by a relative error of at most 0.0065.
Values may be sent and summed in bfloat16 or wider, within the bound.
A program may use at most 384 MiB of HBM per device.

```python
import jax
import jax.numpy as jnp
from jax import lax

D = 8192
QH = 64
KVH = 8
HD = 128
LEN = 4096
STEPS = 4
CANDS = 2
TOKENS = 8192
ROWS = 64


def serving_plan(key):
    plan_keys = jax.random.split(jax.random.fold_in(key, 404), 5)
    full_cand = jax.random.randint(plan_keys[0], (), 0, CANDS)
    cand_ids = jnp.arange(CANDS)
    drawn_lengths = jnp.where(cand_ids == full_cand, LEN, jax.random.randint(plan_keys[1], (CANDS,), LEN // 4, LEN + 1))
    row_order = jax.random.permutation(plan_keys[2], ROWS)
    row_cands = jax.random.randint(plan_keys[3], (ROWS,), 0, CANDS)
    row_cands = row_cands.at[row_order[:CANDS]].set(cand_ids)
    full_row = row_order[full_cand]
    limits = jnp.take(drawn_lengths, row_cands)
    drawn_pos = jax.random.randint(plan_keys[4], (ROWS,), 1, limits + 1)
    drawn_pos = jnp.where(jnp.arange(ROWS) == full_row, LEN, drawn_pos)
    return (drawn_lengths.astype(jnp.int32), row_cands.astype(jnp.int32), drawn_pos.astype(jnp.int32))


def draw_lengths(key, part):
    return serving_plan(key)[0]


def draw_row_cand(key, part):
    return serving_plan(key)[1]


def draw_positions(key, part):
    return serving_plan(key)[2]


def draw_prefill_q(key, part):
    key = jax.random.fold_in(key, 11)
    noise_key = jax.random.fold_in(key, 0)
    drawn_values = 2.0 * jnp.clip(jax.random.normal(noise_key, (TOKENS, QH * HD), jnp.float32), -6.0, 6.0)
    return drawn_values.astype(jnp.bfloat16)


def draw_prefill_kv(key, part):
    key = jax.random.fold_in(key, 12)
    noise_key, value_key = jax.random.split(key, 2)
    key_values = jnp.clip(jax.random.normal(noise_key, (TOKENS, KVH * HD), jnp.float32), -6.0, 6.0)
    value_values = jnp.clip(jax.random.normal(value_key, (TOKENS, KVH * HD), jnp.float32), -6.0, 6.0)
    return jnp.stack([key_values, value_values], axis=1).astype(jnp.bfloat16)


def draw_decode_q(key, part):
    key = jax.random.fold_in(key, 13)
    noise_key = jax.random.fold_in(key, 0)
    drawn_values = 2.0 * jnp.clip(jax.random.normal(noise_key, (ROWS * STEPS, QH * HD), jnp.float32), -6.0, 6.0)
    return drawn_values.reshape(ROWS, STEPS, QH * HD).astype(jnp.bfloat16)


def draw_decode_kv(key, part):
    key = jax.random.fold_in(key, 14)
    drawn_values = jnp.clip(jax.random.normal(key, (ROWS * STEPS, 2, KVH * HD), jnp.float32), -6.0, 6.0)
    return drawn_values.reshape(ROWS, STEPS, 2, KVH * HD).astype(jnp.bfloat16)


def levels(rng, dims, pieces, least, top_value):
    loudness, own = 1.0, jax.random.fold_in(rng, 6)
    for axis_at, shards_of in pieces:
        heights = jnp.exp(jax.random.uniform(jax.random.fold_in(own, axis_at), (shards_of,), jnp.float32, least / len(pieces), top_value / len(pieces)))
        loudness = loudness * jnp.repeat(heights, dims[axis_at] // shards_of).reshape([-1 if axis == axis_at else 1 for axis in range(len(dims))])
    return loudness


def noise(stream_key, dims, width, bound, shards=(), held_as=jnp.bfloat16):
    array = jax.random.normal(stream_key, dims, jnp.float32) * width
    if len(shards) > 0:
        array = levels(stream_key, dims, shards, -0.22, 0.18) * array
    return jnp.clip(array, min=-bound, max=bound).astype(held_as)


def setup_inputs(seed: int = 0, part: int = 0) -> dict:
    splits = jax.random.split(jax.random.key(seed), 9)
    part_keys = jax.random.split(jax.random.fold_in(splits[8], part), 9)
    prefill_q = draw_prefill_q(jax.random.fold_in(jax.random.fold_in(splits[8], part), 71), part)
    prefill_kv = draw_prefill_kv(jax.random.fold_in(jax.random.fold_in(splits[8], part), 71), part)
    lengths = draw_lengths(jax.random.fold_in(jax.random.fold_in(splits[8], part), 71), part)
    decode_q = draw_decode_q(jax.random.fold_in(jax.random.fold_in(splits[8], part), 71), part)
    decode_kv = draw_decode_kv(jax.random.fold_in(jax.random.fold_in(splits[8], part), 71), part)
    row_cand = draw_row_cand(jax.random.fold_in(jax.random.fold_in(splits[8], part), 71), part)
    positions = draw_positions(jax.random.fold_in(jax.random.fold_in(splits[8], part), 71), part)
    out_weight = noise(splits[7], (QH * HD, D), (QH * HD) ** -0.5, 0.0625, ((0, 2), (1, 8)))
    return dict(prefill_q=prefill_q, prefill_kv=prefill_kv, lengths=lengths, decode_q=decode_q, decode_kv=decode_kv, row_cand=row_cand, positions=positions, out_weight=out_weight)


masked_score = -1e30


def prefill_item(item_parts):
    queries, key_rows, value_rows, limit = item_parts
    scaling = HD ** -0.5
    block_rows = min(LEN, 1024)
    outputs = []
    for block_no in range(LEN // block_rows):
        upper_end = (block_no + 1) * block_rows
        query_float = queries[block_no * block_rows:upper_end].astype(jnp.float32)
        scores = jnp.einsum('qgd,td->gqt', query_float, key_rows[:upper_end].astype(jnp.float32)) * scaling
        query_pos = block_no * block_rows + jnp.arange(block_rows)
        key_pos = jnp.arange(upper_end)
        visible = (key_pos[None, :] <= query_pos[:, None]) & (key_pos[None, :] < limit)
        scores = jnp.where(visible[None], scores, masked_score)
        highest = jnp.max(scores, axis=-1, keepdims=True)
        weights = jnp.where(visible[None], jnp.exp(scores - highest), 0.0)
        row_total = jnp.sum(weights, axis=-1)
        rounded = lax.optimization_barrier(weights.astype(jnp.bfloat16)).astype(jnp.float32)
        summed = jnp.einsum('gqt,td->gqd', rounded, value_rows[:upper_end].astype(jnp.float32))
        result = summed / row_total[..., None]
        result = jnp.where((query_pos < limit)[None, :, None], result, 0.0)
        outputs.append(result)
    return jnp.concatenate(outputs, axis=1)


def reference(prefill_q, prefill_kv, lengths, decode_q, decode_kv, row_cand, positions, out_weight):
    group_size = QH // KVH
    scaling = HD ** -0.5
    queries = prefill_q.reshape(CANDS, LEN, KVH, group_size, HD).transpose(0, 2, 1, 3, 4).reshape(CANDS * KVH, LEN, group_size, HD)
    cache_rows = prefill_kv.reshape(CANDS, LEN, 2, KVH, HD).transpose(0, 3, 2, 1, 4).reshape(CANDS * KVH, 2, LEN, HD)
    limits = jnp.repeat(lengths, KVH)
    results = lax.map(prefill_item, (queries, cache_rows[:, 0], cache_rows[:, 1], limits))
    prefill_out = results.reshape(CANDS, KVH, group_size, LEN, HD).transpose(0, 3, 1, 2, 4).reshape(TOKENS, QH * HD).astype(jnp.bfloat16)

    token_index = jnp.arange(TOKENS)
    token_cand = token_index // LEN
    token_pos = token_index % LEN
    seen_mask = (token_cand[None, :] == row_cand[:, None]) & (token_pos[None, :] < positions[:, None])
    causal = jnp.arange(STEPS)[None, :] <= jnp.arange(STEPS)[:, None]
    dec_queries = decode_q.reshape(ROWS, STEPS, KVH, group_size, HD).transpose(2, 0, 1, 3, 4)
    dec_new = decode_kv.reshape(ROWS, STEPS, 2, KVH, HD).transpose(3, 2, 0, 1, 4)
    full_cache = prefill_kv.reshape(TOKENS, 2, KVH, HD).transpose(2, 1, 0, 3)

    def decode_item(item_parts):
        queries_head, new_head, cache_head = item_parts
        query_float = queries_head.astype(jnp.float32)
        old_scores = jnp.einsum('rsgd,td->rsgt', query_float, cache_head[0].astype(jnp.float32)) * scaling
        old_scores = jnp.where(seen_mask[:, None, None, :], old_scores, masked_score)
        new_scores = jnp.einsum('rsgd,rtd->rsgt', query_float, new_head[0].astype(jnp.float32)) * scaling
        new_scores = jnp.where(causal[None, :, None, :], new_scores, masked_score)
        highest = jnp.maximum(jnp.max(old_scores, axis=-1), jnp.max(new_scores, axis=-1))[..., None]
        old_weights = jnp.where(seen_mask[:, None, None, :], jnp.exp(old_scores - highest), 0.0)
        new_weights = jnp.where(causal[None, :, None, :], jnp.exp(new_scores - highest), 0.0)
        row_total = jnp.sum(old_weights, axis=-1) + jnp.sum(new_weights, axis=-1)
        old_rounded = lax.optimization_barrier(old_weights.astype(jnp.bfloat16)).astype(jnp.float32)
        new_rounded = lax.optimization_barrier(new_weights.astype(jnp.bfloat16)).astype(jnp.float32)
        summed = jnp.einsum('rsgt,td->rsgd', old_rounded, cache_head[1].astype(jnp.float32))
        summed = summed + jnp.einsum('rsgt,rtd->rsgd', new_rounded, new_head[1].astype(jnp.float32))
        return summed / row_total[..., None]

    attention = lax.map(decode_item, (dec_queries, dec_new, full_cache))
    attention_rows = attention.transpose(1, 2, 0, 3, 4).reshape(ROWS, STEPS, QH * HD).astype(jnp.bfloat16)
    decoded = jnp.dot(attention_rows.reshape(ROWS * STEPS, QH * HD), out_weight, preferred_element_type=jnp.float32)
    decoded = decoded.reshape(ROWS, STEPS, D).astype(jnp.bfloat16)
    return (prefill_out, decoded)
```

```python
import functools
import math

import jax
import jax.numpy as jnp
from jax import lax
from jax.experimental import pallas as pl
from jax.experimental.pallas import tpu as pltpu
from jax.sharding import PartitionSpec as P

HD = 128
LEN = 4096
TQ = 256
masked_score = -1e30
SCALE2 = math.log2(math.e) * HD ** (-0.5)


def scores_of(queries, keys):
    return lax.dot_general(
        queries, keys, (((1,), (1,)), ((), ())), preferred_element_type=jnp.float32
    )


def with_ones(values):
    return jnp.concatenate([values, jnp.ones_like(values)], axis=1)


def absorb(highest_ref, sums_ref, rows, scores, values):
    old = highest_ref[rows, :1]
    new = jnp.maximum(old, jnp.max(scores, axis=1, keepdims=True))
    weights = jnp.exp2((scores - new) * SCALE2).astype(jnp.bfloat16)
    rescale = jnp.exp2((old - new) * SCALE2)
    sums_ref[rows, :] = sums_ref[rows, :] * rescale + jnp.dot(
        weights, with_ones(values), preferred_element_type=jnp.float32
    )
    highest_ref[rows, :] = jnp.broadcast_to(new, (new.shape[0], HD))


def start(highest_ref, sums_ref):
    highest_ref[...] = jnp.full(highest_ref.shape, masked_score, jnp.float32)
    sums_ref[...] = jnp.zeros(sums_ref.shape, jnp.float32)


def near_kernel(place, q, k_own, v_own, k_mate, v_mate, out, lse, highest, sums):
    tokens = q.shape[0]
    tile = min(TQ, tokens)
    start(highest, sums)

    @pl.when(place[0] == 1)
    def _():
        for at in range(0, tokens, tile):
            absorb(
                highest, sums, pl.ds(at, tile), scores_of(q[pl.ds(at, tile), :], k_mate[...]), v_mate[...]
            )

    for at in range(0, tokens, tile):
        rows = pl.ds(at, tile)
        scores = scores_of(q[rows, :], k_own[: at + tile, :])
        shape = scores.shape
        seen = lax.broadcasted_iota(jnp.int32, shape, 1) <= at + lax.broadcasted_iota(
            jnp.int32, shape, 0
        )
        absorb(highest, sums, rows, jnp.where(seen, scores, masked_score), v_own[: at + tile, :])
        total = sums[rows, HD:]
        out[rows, :] = sums[rows, :HD] / total
        lse[rows, :] = highest[rows, :] + jnp.log2(total) * (1.0 / SCALE2)


def far_kernel(place, q, k_one, v_one, k_two, v_two, near, lse, out, highest, sums):
    tokens = q.shape[0]
    tile = min(TQ, tokens)
    chips, limit = place[1], place[2]
    highest[...] = lse[...]
    sums[:, :HD] = near[...]
    sums[:, HD:] = jnp.ones((tokens, HD), jnp.float32)

    @pl.loop(0, chips)
    def _(chip):
        keys = pl.ds(pl.multiple_of(chip * tokens, tokens), tokens)
        for k, v in ((k_one, v_one), (k_two, v_two)):
            for at in range(0, tokens, tile):
                rows = pl.ds(at, tile)
                absorb(highest, sums, rows, scores_of(q[rows, :], k[keys, :]), v[keys, :])

    position = place[3] + lax.broadcasted_iota(jnp.int32, (tokens, HD), 0)
    attended = sums[:, :HD] / sums[:, HD:]
    out[...] = jnp.where(position < limit, attended, 0.0).astype(out.dtype)


def decode_kernel(
    group, steps, place, q, k_new, v_new, k_own, v_own, k_mate, v_mate,
    k_one, v_one, k_two, v_two, limits, out, highest, sums,
):
    tokens = k_own.shape[0]
    count = q.shape[0]
    queries = jnp.concatenate([q[:, h * HD : (h + 1) * HD] for h in range(group)], axis=0)
    start(highest, sums)
    every = pl.ds(0, group * count)
    shape = (group * count, count)
    asked = lax.rem(lax.broadcasted_iota(jnp.int32, shape, 0), count)
    key = lax.broadcasted_iota(jnp.int32, shape, 1)
    seen = (lax.div(asked, steps) == lax.div(key, steps)) & (key <= asked)
    absorb(
        highest, sums, every,
        jnp.where(seen, scores_of(queries, k_new[...]), masked_score), v_new[...],
    )
    limit = jnp.concatenate([limits[:, :1]] * group, axis=0)

    def block(k, v, keys, base):
        scores = scores_of(queries, k[keys, :])
        position = base + lax.broadcasted_iota(jnp.int32, scores.shape, 1)
        absorb(
            highest, sums, every, jnp.where(position < limit, scores, masked_score), v[keys, :]
        )

    block(k_own, v_own, pl.ds(0, tokens), place[0])
    block(k_mate, v_mate, pl.ds(0, tokens), place[1])

    @pl.loop(0, k_one.shape[0] // tokens)
    def _(chip):
        keys = pl.ds(pl.multiple_of(chip * tokens, tokens), tokens)
        block(k_one, v_one, keys, place[2 + 2 * chip])
        block(k_two, v_two, keys, place[3 + 2 * chip])

    for h in range(group):
        rows = pl.ds(h * count, count)
        out[:, h * HD : (h + 1) * HD] = (sums[rows, :HD] / sums[rows, HD:]).astype(out.dtype)


def column(rows, at, width=HD):
    return pl.BlockSpec((rows, width), lambda h, place: (0, at(h)))


def body(mesh_shape, prefill_q, prefill_kv, lengths, decode_q, decode_kv, row_cand, positions, out_weight):
    tokens = prefill_q.shape[0]
    heads = prefill_q.shape[1] // HD
    width = prefill_kv.shape[2]
    kv_heads = width // HD
    group = heads // kv_heads
    seqs, sections = mesh_shape["seq"], mesh_shape["section"]
    chips = LEN // (tokens * sections)
    shards = chips * sections
    z, section = lax.axis_index("seq"), lax.axis_index("section")
    cand, chip = z // chips, z % chips
    row_count, steps = decode_q.shape[:2]
    count = row_count * steps

    kv = prefill_kv.reshape(tokens, 2 * width)
    swap = [(i, sections - 1 - i) for i in range(sections)]
    mate = lax.ppermute(kv, "section", swap)
    ones = [
        lax.ppermute(
            kv, "seq", [(i, i // chips * chips + (i % chips + d) % chips) for i in range(seqs)]
        )
        for d in range(1, chips)
    ]
    spread = [
        (j * sections + c, c * shards + j) for j in range(seqs) for c in range(sections)
    ]
    new = jnp.concatenate(
        [decode_q.reshape(count, -1), decode_kv.reshape(count, -1)], axis=1
    )
    new = lax.ppermute(new, ("seq", "section"), spread)
    all_cands = lax.all_gather(row_cand, "seq", axis=0, tiled=True)
    all_limits = lax.all_gather(positions, "seq", axis=0, tiled=True)
    limit = jnp.sum(jnp.where(jnp.arange(lengths.shape[0]) == cand, lengths, 0))
    start_at = (chip * sections + section) * tokens
    place = jnp.stack([section, chip, limit, start_at]).astype(jnp.int32)

    block_ops = tokens * tokens * HD * heads * 4
    params = pltpu.CompilerParams(
        dimension_semantics=("arbitrary",), vmem_limit_bytes=56 * 2**20
    )
    of_query = column(tokens, lambda h: h)
    of_key = column(tokens, lambda h: h // group)
    of_value = column(tokens, lambda h: kv_heads + h // group)
    state = [pltpu.VMEM((tokens, HD), jnp.float32), pltpu.VMEM((tokens, 2 * HD), jnp.float32)]
    near, lse = pl.pallas_call(
        near_kernel,
        out_shape=[jax.ShapeDtypeStruct((tokens, heads * HD), jnp.float32)] * 2,
        grid_spec=pltpu.PrefetchScalarGridSpec(
            num_scalar_prefetch=1,
            grid=(heads,),
            in_specs=[of_query, of_key, of_value, of_key, of_value],
            out_specs=[of_query, of_query],
            scratch_shapes=state,
        ),
        compiler_params=params,
        cost_estimate=pl.CostEstimate(
            flops=3 * block_ops, bytes_accessed=2**26, transcendentals=0
        ),
        name="near",
    )(place, prefill_q, kv, kv, mate, mate)

    one = jnp.concatenate(ones, axis=0) if len(ones) > 1 else ones[0]
    two = lax.ppermute(one, "section", swap)

    slot = chip * sections + section
    my_cands = lax.dynamic_slice_in_dim(all_cands, slot * row_count, row_count)
    my_limits = lax.dynamic_slice_in_dim(all_limits, slot * row_count, row_count)
    my_limits = jnp.repeat(jnp.where(my_cands == cand, my_limits, 0), steps)
    bases = [start_at, (chip * sections + 1 - section) * tokens]
    for d in range(1, chips):
        other = (chip - d) % chips
        bases += [(other * sections + section) * tokens, (other * sections + 1 - section) * tokens]
    far_rows = one.shape[0]
    key_at, value_at = (lambda h: h), (lambda h: kv_heads + h)
    new_at = heads
    decode_out = pl.pallas_call(
        functools.partial(decode_kernel, group, steps),
        out_shape=jax.ShapeDtypeStruct((count, heads * HD), jnp.bfloat16),
        grid_spec=pltpu.PrefetchScalarGridSpec(
            num_scalar_prefetch=1,
            grid=(kv_heads,),
            in_specs=[
                column(count, lambda h: h, group * HD),
                column(count, lambda h: new_at + h),
                column(count, lambda h: new_at + kv_heads + h),
                column(tokens, key_at), column(tokens, value_at),
                column(tokens, key_at), column(tokens, value_at),
                column(far_rows, key_at), column(far_rows, value_at),
                column(far_rows, key_at), column(far_rows, value_at),
                pl.BlockSpec((count, HD), lambda h, place: (0, 0)),
            ],
            out_specs=column(count, lambda h: h, group * HD),
            scratch_shapes=[
                pltpu.VMEM((group * count, HD), jnp.float32),
                pltpu.VMEM((group * count, 2 * HD), jnp.float32),
            ],
        ),
        compiler_params=params,
        cost_estimate=pl.CostEstimate(
            flops=2 * count * LEN * HD * heads * 4, bytes_accessed=2**24, transcendentals=0
        ),
        name="decode",
    )(
        jnp.stack(bases).astype(jnp.int32), new, new, new, kv, kv, mate, mate,
        one, one, two, two, jnp.broadcast_to(my_limits[:, None], (count, HD)),
    )
    every = lax.all_gather(decode_out, ("seq", "section"), axis=0, tiled=False)

    of_far_key = column(far_rows, lambda h: h // group)
    of_far_value = column(far_rows, lambda h: kv_heads + h // group)
    prefill_out = pl.pallas_call(
        far_kernel,
        out_shape=jax.ShapeDtypeStruct((tokens, heads * HD), jnp.bfloat16),
        grid_spec=pltpu.PrefetchScalarGridSpec(
            num_scalar_prefetch=1,
            grid=(heads,),
            in_specs=[
                of_query, of_far_key, of_far_value, of_far_key, of_far_value, of_query, of_query,
            ],
            out_specs=of_query,
            scratch_shapes=state,
        ),
        compiler_params=params,
        cost_estimate=pl.CostEstimate(
            flops=4 * block_ops, bytes_accessed=2**26, transcendentals=0
        ),
        name="far",
    )(place, prefill_q, one, one, two, two, near, lse)

    every = every.reshape(-1, shards * count, heads * HD)
    chosen = jnp.repeat(all_cands, steps)[:, None]
    rows = every[0]
    for c in range(1, every.shape[0]):
        rows = jnp.where(chosen == c, every[c], rows)
    terms = jnp.dot(rows, out_weight, preferred_element_type=jnp.float32)
    decoded = lax.psum_scatter(terms, "heads", scatter_dimension=0, tiled=True)
    decoded = decoded.astype(jnp.bfloat16).reshape(-1, steps, out_weight.shape[1])
    return (prefill_out, decoded)


def solution(mesh):
    return jax.shard_map(
        functools.partial(body, dict(mesh.shape)),
        mesh=mesh,
        in_specs=(
            P(("groups", "seq", "section"), "heads"),
            P(("groups", "seq", "section"), None, "heads"),
            P("groups"),
            P(("groups", "seq"), None, "heads"),
            P(("groups", "seq"), None, None, "heads"),
            P(("groups", "seq")),
            P(("groups", "seq")),
            P("heads", ("seq", "section")),
        ),
        out_specs=(
            P(("groups", "seq", "section"), "heads"),
            P(("groups", "heads"), None, ("seq", "section")),
        ),
        check_vma=False,
    )
```

```python
import functools
import math

import jax
import jax.numpy as jnp
from jax import lax
from jax.experimental import pallas as pl
from jax.experimental.pallas import tpu as pltpu
from jax.sharding import PartitionSpec as P

HD = 128
LEN = 4096
TQ = 256
masked_score = -1e30
SCALE2 = math.log2(math.e) * HD ** (-0.5)


def scores_of(queries, keys):
    return lax.dot_general(
        queries, keys, (((1,), (1,)), ((), ())), preferred_element_type=jnp.float32
    )


def with_ones(values):
    return jnp.concatenate([values, jnp.ones_like(values)], axis=1)


def absorb(highest_ref, sums_ref, rows, scores, values):
    old = highest_ref[rows, :1]
    new = jnp.maximum(old, jnp.max(scores, axis=1, keepdims=True))
    weights = jnp.exp2((scores - new) * SCALE2).astype(jnp.bfloat16)
    rescale = jnp.exp2((old - new) * SCALE2)
    sums_ref[rows, :] = sums_ref[rows, :] * rescale + jnp.dot(
        weights, with_ones(values), preferred_element_type=jnp.float32
    )
    highest_ref[rows, :] = jnp.broadcast_to(new, (new.shape[0], HD))


def start(highest_ref, sums_ref):
    highest_ref[...] = jnp.full(highest_ref.shape, masked_score, jnp.float32)
    sums_ref[...] = jnp.zeros(sums_ref.shape, jnp.float32)


def near_kernel(place, q, k_own, v_own, k_mate, v_mate, out, lse):
    tokens = q.shape[0]
    tile = min(TQ, tokens)

    def attend(with_mate):
        for at in range(0, tokens, tile):
            rows = pl.ds(at, tile)
            queries = q[rows, :]
            last = scores_of(queries, k_own[rows, :])
            seen = lax.broadcasted_iota(jnp.int32, last.shape, 1) <= lax.broadcasted_iota(
                jnp.int32, last.shape, 0
            )
            blocks = [(jnp.where(seen, last, masked_score), v_own[rows, :])]
            if at > 0:
                blocks.append((scores_of(queries, k_own[:at, :]), v_own[:at, :]))
            if with_mate:
                blocks.append((scores_of(queries, k_mate[...]), v_mate[...]))
            tops = [jnp.max(scores, axis=1, keepdims=True) for scores, _ in blocks]
            top = functools.reduce(jnp.maximum, tops)
            sums = sum(
                jnp.dot(
                    jnp.exp2((scores - top) * SCALE2).astype(jnp.bfloat16),
                    with_ones(values),
                    preferred_element_type=jnp.float32,
                )
                for scores, values in blocks
            )
            total = sums[:, HD:]
            out[rows, :] = sums[:, :HD] / total
            lse[rows, :] = top + jnp.log2(total) * (1.0 / SCALE2)

    @pl.when(place[0] == 1)
    def _():
        attend(True)

    @pl.when(place[0] != 1)
    def _():
        attend(False)


def far_kernel(place, q, k_one, v_one, k_two, v_two, near, lse, *rest):
    out, highest, sums = rest[-3:]
    tokens = q.shape[0]
    tile = min(TQ, tokens)
    chips, limit = place[1], place[2]
    highest[...] = lse[...]
    sums[:, :HD] = near[...]
    sums[:, HD:] = jnp.ones((tokens, HD), jnp.float32)

    @pl.loop(0, chips)
    def _(chip):
        keys = pl.ds(pl.multiple_of(chip * tokens, tokens), tokens)
        for k, v in ((k_one, v_one), (k_two, v_two)):
            for at in range(0, tokens, tile):
                rows = pl.ds(at, tile)
                absorb(highest, sums, rows, scores_of(q[rows, :], k[keys, :]), v[keys, :])

    position = place[3] + lax.broadcasted_iota(jnp.int32, (tokens, HD), 0)
    attended = sums[:, :HD] / sums[:, HD:]
    out[...] = jnp.where(position < limit, attended, 0.0).astype(out.dtype)


def decode_kernel(
    group, steps, place, q, k_new, v_new, k_own, v_own, k_mate, v_mate,
    k_one, v_one, k_two, v_two, limits, out, highest, sums,
):
    tokens = k_own.shape[0]
    count = q.shape[0]
    queries = jnp.concatenate([q[:, h * HD : (h + 1) * HD] for h in range(group)], axis=0)
    start(highest, sums)
    half = 2 * count
    shape = (half, count)
    asked = lax.rem(lax.broadcasted_iota(jnp.int32, shape, 0), count)
    key = lax.broadcasted_iota(jnp.int32, shape, 1)
    seen = (lax.div(asked, steps) == lax.div(key, steps)) & (key <= asked)
    limit = jnp.concatenate([limits[:, :1]] * 2, axis=0)
    for at in range(0, group * count, half):
        scores = scores_of(queries[at : at + half], k_new[...])
        absorb(highest, sums, pl.ds(at, half), jnp.where(seen, scores, masked_score), v_new[...])

    def block(k, v, keys, base):
        for at in range(0, group * count, half):
            scores = scores_of(queries[at : at + half], k[keys, :])
            position = base + lax.broadcasted_iota(jnp.int32, scores.shape, 1)
            scores = jnp.where(position < limit, scores, masked_score)
            absorb(highest, sums, pl.ds(at, half), scores, v[keys, :])

    block(k_own, v_own, pl.ds(0, tokens), place[0])
    block(k_mate, v_mate, pl.ds(0, tokens), place[1])

    @pl.loop(0, k_one.shape[0] // tokens)
    def _(chip):
        keys = pl.ds(pl.multiple_of(chip * tokens, tokens), tokens)
        block(k_one, v_one, keys, place[2 + 2 * chip])
        block(k_two, v_two, keys, place[3 + 2 * chip])

    for h in range(group):
        rows = pl.ds(h * count, count)
        out[:, h * HD : (h + 1) * HD] = (sums[rows, :HD] / sums[rows, HD:]).astype(out.dtype)


def column(rows, at, width=HD):
    return pl.BlockSpec((rows, width), lambda h, place: (0, at(h)))


def body(mesh_shape, prefill_q, prefill_kv, lengths, decode_q, decode_kv, row_cand, positions, out_weight):
    tokens = prefill_q.shape[0]
    heads = prefill_q.shape[1] // HD
    width = prefill_kv.shape[2]
    kv_heads = width // HD
    group = heads // kv_heads
    seqs, sections = mesh_shape["seq"], mesh_shape["section"]
    chips = LEN // (tokens * sections)
    shards = chips * sections
    z, section = lax.axis_index("seq"), lax.axis_index("section")
    cand, chip = z // chips, z % chips
    row_count, steps = decode_q.shape[:2]
    count = row_count * steps

    kv = prefill_kv.reshape(tokens, 2 * width)
    swap = [(i, sections - 1 - i) for i in range(sections)]
    mate = lax.ppermute(kv, "section", swap)
    ones = [
        lax.ppermute(
            kv, "seq", [(i, i // chips * chips + (i % chips + d) % chips) for i in range(seqs)]
        )
        for d in range(1, chips)
    ]
    spread = [
        (j * sections + c, c * shards + j) for j in range(seqs) for c in range(sections)
    ]
    new = jnp.concatenate(
        [decode_q.reshape(count, -1), decode_kv.reshape(count, -1)], axis=1
    )
    new = lax.ppermute(new, ("seq", "section"), spread)
    all_cands = lax.all_gather(row_cand, "seq", axis=0, tiled=True)
    all_limits = lax.all_gather(positions, "seq", axis=0, tiled=True)
    limit = jnp.sum(jnp.where(jnp.arange(lengths.shape[0]) == cand, lengths, 0))
    start_at = (chip * sections + section) * tokens
    place = jnp.stack([section, chip, limit, start_at]).astype(jnp.int32)

    block_ops = tokens * tokens * HD * heads * 4
    params = pltpu.CompilerParams(
        dimension_semantics=("arbitrary",), vmem_limit_bytes=56 * 2**20
    )
    of_query = column(tokens, lambda h: h)
    of_key = column(tokens, lambda h: h // group)
    of_value = column(tokens, lambda h: kv_heads + h // group)
    state = [pltpu.VMEM((tokens, HD), jnp.float32), pltpu.VMEM((tokens, 2 * HD), jnp.float32)]
    near, lse = pl.pallas_call(
        near_kernel,
        out_shape=[jax.ShapeDtypeStruct((tokens, heads * HD), jnp.float32)] * 2,
        grid_spec=pltpu.PrefetchScalarGridSpec(
            num_scalar_prefetch=1,
            grid=(heads,),
            in_specs=[of_query, of_key, of_value, of_key, of_value],
            out_specs=[of_query, of_query],
        ),
        compiler_params=params,
        cost_estimate=pl.CostEstimate(
            flops=3 * block_ops, bytes_accessed=2**26, transcendentals=0
        ),
        name="near",
    )(place, prefill_q, kv, kv, mate, mate)

    near, lse, new, ones, all_cands, all_limits = lax.optimization_barrier(
        (near, lse, new, ones, all_cands, all_limits)
    )
    one = jnp.concatenate(ones, axis=0) if len(ones) > 1 else ones[0]
    two = lax.ppermute(one, "section", swap)

    slot = chip * sections + section
    my_cands = lax.dynamic_slice_in_dim(all_cands, slot * row_count, row_count)
    my_limits = lax.dynamic_slice_in_dim(all_limits, slot * row_count, row_count)
    my_limits = jnp.repeat(jnp.where(my_cands == cand, my_limits, 0), steps)
    bases = [start_at, (chip * sections + 1 - section) * tokens]
    for d in range(1, chips):
        other = (chip - d) % chips
        bases += [(other * sections + section) * tokens, (other * sections + 1 - section) * tokens]
    far_rows = one.shape[0]
    key_at, value_at = (lambda h: h), (lambda h: kv_heads + h)
    new_at = heads
    decode_out = pl.pallas_call(
        functools.partial(decode_kernel, group, steps),
        out_shape=jax.ShapeDtypeStruct((count, heads * HD), jnp.bfloat16),
        grid_spec=pltpu.PrefetchScalarGridSpec(
            num_scalar_prefetch=1,
            grid=(kv_heads,),
            in_specs=[
                column(count, lambda h: h, group * HD),
                column(count, lambda h: new_at + h),
                column(count, lambda h: new_at + kv_heads + h),
                column(tokens, key_at), column(tokens, value_at),
                column(tokens, key_at), column(tokens, value_at),
                column(far_rows, key_at), column(far_rows, value_at),
                column(far_rows, key_at), column(far_rows, value_at),
                pl.BlockSpec((count, HD), lambda h, place: (0, 0)),
            ],
            out_specs=column(count, lambda h: h, group * HD),
            scratch_shapes=[
                pltpu.VMEM((group * count, HD), jnp.float32),
                pltpu.VMEM((group * count, 2 * HD), jnp.float32),
            ],
        ),
        compiler_params=params,
        cost_estimate=pl.CostEstimate(
            flops=2 * count * LEN * HD * heads * 4, bytes_accessed=2**24, transcendentals=0
        ),
        name="decode",
    )(
        jnp.stack(bases).astype(jnp.int32), new, new, new, kv, kv, mate, mate,
        one, one, two, two, jnp.broadcast_to(my_limits[:, None], (count, HD)),
    )
    every = lax.all_gather(decode_out, ("seq", "section"), axis=0, tiled=False)

    def far(place, first, number, earlier):
        head = lambda h: first + h
        of_query = column(tokens, head)
        of_far_key = column(far_rows, lambda h: head(h) // group)
        of_far_value = column(far_rows, lambda h: kv_heads + head(h) // group)
        return pl.pallas_call(
            far_kernel,
            out_shape=jax.ShapeDtypeStruct((tokens, heads * HD), jnp.bfloat16),
            grid_spec=pltpu.PrefetchScalarGridSpec(
                num_scalar_prefetch=1,
                grid=(number,),
                in_specs=[
                    of_query, of_far_key, of_far_value, of_far_key, of_far_value, of_query, of_query,
                ]
                + [pl.BlockSpec(memory_space=pl.ANY)] * len(earlier),
                out_specs=of_query,
                scratch_shapes=state,
            ),
            input_output_aliases={8: 0} if earlier else {},
            compiler_params=params,
            cost_estimate=pl.CostEstimate(
                flops=4 * block_ops * number // heads, bytes_accessed=2**25, transcendentals=0
            ),
            name="far",
        )(place, prefill_q, one, one, two, two, near, lse, *earlier)

    first = heads // 2
    prefill_out = far(place, 0, first, [])
    every, prefill_out = lax.optimization_barrier((every, prefill_out))
    every = every.reshape(-1, shards * count, heads * HD)
    chosen = jnp.repeat(all_cands, steps)[:, None]
    rows = every[0]
    for c in range(1, every.shape[0]):
        rows = jnp.where(chosen == c, every[c], rows)
    terms = jnp.dot(rows, out_weight, preferred_element_type=jnp.float32)
    terms, place = lax.optimization_barrier((terms, place))
    prefill_out = far(place, first, heads - first, [prefill_out])
    decoded = lax.psum_scatter(terms, "heads", scatter_dimension=0, tiled=True)
    decoded = decoded.astype(jnp.bfloat16).reshape(-1, steps, out_weight.shape[1])
    return (prefill_out, decoded)


def solution(mesh):
    return jax.shard_map(
        functools.partial(body, dict(mesh.shape)),
        mesh=mesh,
        in_specs=(
            P(("groups", "seq", "section"), "heads"),
            P(("groups", "seq", "section"), None, "heads"),
            P("groups"),
            P(("groups", "seq"), None, "heads"),
            P(("groups", "seq"), None, None, "heads"),
            P(("groups", "seq")),
            P(("groups", "seq")),
            P("heads", ("seq", "section")),
        ),
        out_specs=(
            P(("groups", "seq", "section"), "heads"),
            P(("groups", "heads"), None, ("seq", "section")),
        ),
        check_vma=False,
    )
```
